32 devices in a mesh: seq: 8 (over y, x, core), head: 4 (over z).
Axes of the slice: x: 2, y: 2, z: 4, core: 2. Of those that a mesh axis runs over, the one named last changes fastest.
Arguments:
- projected: bfloat16 [12288, 6912], P(('seq', 'head')), may hold values from -10 to 10
- segment_ids: int32 [12288], replicated, may hold values from 0 to 15, never falling along the last dimension, each value on 1 to 1536 neighbouring positions
- widths: int32 [16], replicated, may hold values from 16 to 64
Outputs:
- attended: bfloat16 [12288, 2304], P(('seq', 'head'))
The draws below stay inside these ranges and needn't reach their ends.
Inputs may be any that keep to these rules, and one draw needn't show every extreme that they name: `segment_ids`: ids never fall along the sequence; each of the 16 samples covers 1 to 1536 consecutive positions and some sample covers exactly 1536.
All inputs are finite; a program needn't handle non-finite values.
Results may differ from the reference program's by a relative error of at most 0.0088.
Values may be sent and summed in bfloat16 or wider, within the bound.
A program may use at most 128 MiB of HBM per device.

```python
import math
import jax
import jax.numpy as jnp
import numpy as np
from jax import lax

D = 2304
HEADS = 24
MAXLEN = 1536
TOKENS = 12288
SAMPLES = 16


def draw_projected(key, part):
    head_size = D // HEADS
    base_key = jax.random.fold_in(key, 11)
    shape = (TOKENS, 3, HEADS, head_size)
    stacked = jnp.clip(jax.random.normal(base_key, shape, jnp.float32), -5.0, 5.0)
    return stacked.reshape(TOKENS, 3 * D).astype(jnp.bfloat16)


def with_ends(result, stream_key, smallest, largest):
    shape = result.shape
    spot = [jax.random.randint(jax.random.fold_in(stream_key, axis), (), 0, shape[axis]) for axis in range(len(shape))]
    result = result.at[tuple(spot)].set(smallest)
    longest = shape.index(max(shape))
    spot[longest] = (spot[longest] + 1) % shape[longest]
    return result.at[tuple(spot)].set(largest)


def split_up(count, total, reach, skew):
    portions = [(1 << 20) // math.isqrt(standing ** skew) + 1 for standing in range(2, count + 1)]
    spare, counts = total - reach - (count - 1), [1] * (count - 1)
    while spare > 0:
        movable = [i for i in range(count - 1) if counts[i] < reach]
        pool, budget = sum([portions[i] for i in movable]), spare
        for i in movable:
            addition = min(reach - counts[i], max(1, budget * portions[i] // pool), spare)
            counts[i] = counts[i] + addition
            spare = spare - addition
    return np.array([reach] + counts)


def ragged(key, number_of, total, limit, skew):
    if number_of == 2:
        one = jax.random.randint(key, (), max(1, total - limit), min(limit, total - 1) + 1)
        return jnp.stack([one, total - one])
    sizes = jnp.asarray(split_up(number_of, total, limit, skew), jnp.int32)
    pairs = (number_of - 1) // 2
    giver, receiver = sizes[1:1 + 2 * pairs:2], sizes[2:2 + 2 * pairs:2]
    slack = jnp.minimum(giver - 1, limit - receiver)
    shifted = jax.random.randint(jax.random.fold_in(key, 1), (pairs,), 0, 1 << 20) % (slack + 1)
    sizes = sizes.at[1:1 + 2 * pairs:2].set(giver - shifted).at[2:2 + 2 * pairs:2].set(receiver + shifted)
    return sizes[jax.random.permutation(jax.random.fold_in(key, 2), number_of)]


def setup_inputs(seed: int = 0) -> dict:
    key_list = jax.random.split(jax.random.key(seed), 4)
    projected = draw_projected(jax.random.fold_in(key_list[3], 71), 0)
    segment_ids = jnp.searchsorted(jnp.cumsum(ragged(key_list[1], SAMPLES, TOKENS, MAXLEN, 2)), jnp.arange(TOKENS), side="right").astype(jnp.int32)
    widths = with_ends(jax.random.randint(key_list[2], (SAMPLES,), 16, 65), jax.random.fold_in(key_list[2], 1), 16, 64).astype(jnp.int32)
    return dict(projected=projected, segment_ids=segment_ids, widths=widths)


masked_score = -1e+30

def rotate(head_vals, row_pos, col_pos):
    quarter = head_vals.shape[-1] // 4
    frequency = 10000.0 ** (-jnp.arange(quarter, dtype=jnp.float32) / quarter)

    def turn(half_vals, place):
        angles = place.astype(jnp.float32)[:, None] * frequency[None, :]
        cosine = jnp.cos(angles)[:, None, :]
        sine_part = jnp.sin(angles)[:, None, :]
        first_half = half_vals[..., :quarter]
        second = half_vals[..., quarter:]
        return jnp.concatenate([first_half * cosine - second * sine_part, first_half * sine_part + second * cosine], axis=-1)
    middle = 2 * quarter
    return jnp.concatenate([turn(head_vals[..., :middle], row_pos), turn(head_vals[..., middle:], col_pos)], axis=-1)

def starts_of(segment_ids):
    length = segment_ids.shape[0]
    indices = jnp.arange(length, dtype=jnp.int32)
    before = jnp.concatenate([jnp.full((1,), -1, jnp.int32), segment_ids[:-1]])
    return lax.cummax(jnp.where(segment_ids != before, indices, 0), axis=0)

def reference(projected, segment_ids, widths):
    tokens = projected.shape[0]
    head_size = D // HEADS
    indices = jnp.arange(tokens, dtype=jnp.int32)
    offset = indices - starts_of(segment_ids)
    width_tok = widths[segment_ids]
    row_pos = offset // width_tok
    col_pos = offset % width_tok
    qkv_parts = projected.reshape(tokens, 3, HEADS, head_size)
    queries = rotate(qkv_parts[:, 0].astype(jnp.float32), row_pos, col_pos).astype(jnp.bfloat16)
    key_rows = rotate(qkv_parts[:, 1].astype(jnp.float32), row_pos, col_pos).astype(jnp.bfloat16)
    values = qkv_parts[:, 2]
    reach_rows = MAXLEN
    zero_rows = jnp.zeros((reach_rows, HEADS, head_size), jnp.bfloat16)
    key_pad = jnp.concatenate([zero_rows, key_rows, zero_rows], axis=0)
    value_pad = jnp.concatenate([zero_rows, values, zero_rows], axis=0)
    no_sample = jnp.full((reach_rows,), -1, jnp.int32)
    seg_pad = jnp.concatenate([no_sample, segment_ids, no_sample], axis=0)
    block_rows = min(512, tokens)
    scaling = 1.0 / math.sqrt(head_size)

    def one_block(number):
        start_row = number * block_rows
        q_blk = lax.dynamic_slice_in_dim(queries, start_row, block_rows, 0).astype(jnp.float32)
        k_blk = lax.dynamic_slice_in_dim(key_pad, start_row, block_rows + 2 * reach_rows, 0).astype(jnp.float32)
        v_blk = lax.dynamic_slice_in_dim(value_pad, start_row, block_rows + 2 * reach_rows, 0).astype(jnp.float32)
        q_ids = lax.dynamic_slice_in_dim(segment_ids, start_row, block_rows, 0)
        k_ids = lax.dynamic_slice_in_dim(seg_pad, start_row, block_rows + 2 * reach_rows, 0)
        scores = jnp.einsum('qhe,khe->hqk', q_blk, k_blk) * scaling
        same_seg = (q_ids[:, None] == k_ids[None, :])[None]
        scores = jnp.where(same_seg, scores, masked_score)
        row_max = lax.optimization_barrier(jnp.max(scores, axis=2, keepdims=True))
        weights = jnp.where(same_seg, jnp.exp(scores - row_max), 0.0)
        totals = lax.optimization_barrier(jnp.sum(weights, axis=2, keepdims=True))
        blended = jnp.einsum('hqk,khe->hqe', weights.astype(jnp.bfloat16).astype(jnp.float32), v_blk)
        return jnp.transpose(blended / totals, (1, 0, 2)).astype(jnp.bfloat16)
    results = lax.map(one_block, jnp.arange(tokens // block_rows, dtype=jnp.int32))
    return results.reshape(tokens, D)
```

```python
import functools
import math

import jax
import jax.numpy as jnp
from jax import lax
from jax.experimental import pallas as pl
from jax.experimental.pallas import tpu as pltpu
from jax.sharding import PartitionSpec as P

D = 2304
HEADS = 24
HEAD = D // HEADS
QUARTER = HEAD // 4
ONES = 16
APART = -131072.0
MESH = pl.DeviceIdType.MESH


def transposed(block):
    return jnp.transpose(block.astype(jnp.float32), (1, 0))


def kernel(
    group, chunks, seqs, x_ref, turns_ref, kaug_ref, qaug_ref, out_ref,
    send, held, keys, blended, back,
    in_send, in_recv, in_own, halo_send, halo_recv, back_send, back_recv, back_own,
):
    tok = x_ref.shape[0]
    span = group * HEAD
    aug = kaug_ref.shape[1]
    seq = lax.axis_index("seq")
    me = lax.axis_index("head")
    has_left = seq > 0
    has_right = seq < seqs - 1
    scale = math.log2(math.e) / math.sqrt(HEAD)

    barrier = pltpu.get_barrier_semaphore()
    for d in range(1, group):
        pl.semaphore_signal(
            barrier, inc=1, device_id={"head": lax.rem(me + d, group)}, device_id_type=MESH
        )

    @pl.when(has_left)
    def _():
        pl.semaphore_signal(barrier, inc=1, device_id={"seq": seq - 1}, device_id_type=MESH)

    @pl.when(has_right)
    def _():
        pl.semaphore_signal(barrier, inc=1, device_id={"seq": seq + 1}, device_id_type=MESH)

    pl.semaphore_wait(
        barrier, group - 1 + has_left.astype(jnp.int32) + has_right.astype(jnp.int32)
    )

    def in_copy(j, d):
        dest = lax.rem(me + d, group)
        return pltpu.make_async_remote_copy(
            src_ref=send.at[j, dest],
            dst_ref=held.at[j, group + me],
            send_sem=in_send.at[j, d - 1],
            recv_sem=in_recv.at[j, d - 1],
            device_id={"head": dest},
            device_id_type=MESH,
        )

    def own_copy(j):
        return pltpu.make_async_copy(send.at[j, me], held.at[j, group + me], in_own.at[j])

    def halo_copy(j, side):
        slot = 0 if side == 0 else 2 * group
        return pltpu.make_async_remote_copy(
            src_ref=held.at[j, pl.ds(group, group), pl.ds(1, 2)],
            dst_ref=held.at[j, pl.ds(slot, group), pl.ds(1, 2)],
            send_sem=halo_send.at[j, side],
            recv_sem=halo_recv.at[j, side],
            device_id={"seq": seq + 1 if side == 0 else seq - 1},
            device_id_type=MESH,
        )

    def back_copy(j, d):
        dest = lax.rem(me + d, group)
        return pltpu.make_async_remote_copy(
            src_ref=blended.at[j, dest],
            dst_ref=back.at[j, me],
            send_sem=back_send.at[j, d - 1],
            recv_sem=back_recv.at[j, d - 1],
            device_id={"head": dest},
            device_id_type=MESH,
        )

    def back_own_copy(j):
        return pltpu.make_async_copy(blended.at[j, me], back.at[j, me], back_own.at[j])

    def issue(j):
        for part in range(3):
            first = pl.multiple_of(part * D + j * span, 128)
            cols = transposed(x_ref[:, pl.ds(first, span)])
            for z in range(group):
                vals = cols[z * HEAD:(z + 1) * HEAD]
                if part < 2:
                    pieces = []
                    for half in range(2):
                        cosine, sine = turns_ref[2 * half], turns_ref[2 * half + 1]
                        low = vals[2 * half * QUARTER:(2 * half + 1) * QUARTER]
                        high = vals[(2 * half + 1) * QUARTER:(2 * half + 2) * QUARTER]
                        pieces += [low * cosine - high * sine, low * sine + high * cosine]
                    vals = jnp.concatenate(pieces, axis=0)
                send[j, z, part] = vals.astype(jnp.bfloat16)
        for d in range(1, group):
            in_copy(j, d).start()
        own_copy(j).start()

    def arrive(j):
        own_copy(j).wait()
        for d in range(1, group):
            in_copy(j, d).wait_recv()

        @pl.when(has_right)
        def _():
            halo_copy(j, 0).start()

        @pl.when(has_left)
        def _():
            halo_copy(j, 1).start()

    def halo_arrive(j):
        @pl.when(has_left)
        def _():
            halo_copy(j, 0).wait_recv()

        @pl.when(has_right)
        def _():
            halo_copy(j, 1).wait_recv()

        @pl.when(jnp.logical_not(has_left))
        def _():
            for z in range(group):
                held[j, z] = jnp.zeros((3, HEAD, tok), jnp.bfloat16)

        @pl.when(jnp.logical_not(has_right))
        def _():
            for z in range(group):
                held[j, 2 * group + z] = jnp.zeros((3, HEAD, tok), jnp.bfloat16)

    window = 2 * group + 1
    several = 3 if window % 3 == 0 else 1

    def attend(j):
        def lay(slot, carry):
            joined = jnp.concatenate([held[j, slot, 1], kaug_ref[slot]], axis=0)
            keys[slot] = transposed(joined).astype(jnp.bfloat16)
            return carry

        lax.fori_loop(0, 3 * group, lay, 0)
        ones = jnp.ones((ONES, tok), jnp.bfloat16)

        def query_block(i, carry):
            q = jnp.concatenate([held[j, group + i, 0], qaug_ref[i]], axis=0)

            def key_blocks(step, state):
                top, acc = state
                scores = []
                for b in range(several):
                    scores.append(
                        jnp.dot(keys[i + step * several + b], q, preferred_element_type=jnp.float32)
                    )
                new_top = top
                for s in scores:
                    new_top = jnp.maximum(new_top, jnp.max(s, axis=0, keepdims=True))
                acc = acc * jnp.exp2((top - new_top) * scale)
                for b, s in enumerate(scores):
                    weights = jnp.exp2((s - new_top) * scale).astype(jnp.bfloat16)
                    v = jnp.concatenate([held[j, i + step * several + b, 2], ones], axis=0)
                    acc = acc + jnp.dot(v, weights, preferred_element_type=jnp.float32)
                return new_top, acc

            top = jnp.full((1, tok), -1e30, jnp.float32)
            acc = jnp.zeros((HEAD + ONES, tok), jnp.float32)
            top, acc = lax.fori_loop(0, window // several, key_blocks, (top, acc))
            blended[j, i] = (acc[:HEAD] / acc[HEAD:HEAD + 1]).astype(jnp.bfloat16)
            return carry

        lax.fori_loop(0, group, query_block, 0)
        for d in range(1, group):
            back_copy(j, d).start()
        back_own_copy(j).start()

    issue(0)

    def step(t, carry):
        @pl.when(t + 1 < chunks)
        def _():
            issue(t + 1)

        @pl.when(t < chunks)
        def _():
            arrive(t)

        @pl.when(t >= 1)
        def _():
            halo_arrive(t - 1)
            attend(t - 1)

        return carry

    lax.fori_loop(0, chunks + 1, step, 0)

    def finish(j, carry):
        back_own_copy(j).wait()
        for d in range(1, group):
            back_copy(j, d).wait_recv()
        rows = jnp.concatenate([back[j, z] for z in range(group)], axis=0)
        out_ref[:, pl.ds(pl.multiple_of(j * span, 128), span)] = transposed(rows).astype(
            jnp.bfloat16
        )
        for d in range(1, group):
            in_copy(j, d).wait_send()
            back_copy(j, d).wait_send()

        @pl.when(has_right)
        def _():
            halo_copy(j, 0).wait_send()

        @pl.when(has_left)
        def _():
            halo_copy(j, 1).wait_send()

        return carry

    lax.fori_loop(0, chunks, finish, 0)


def body(projected, segment_ids, widths):
    tok = projected.shape[0]
    group = lax.axis_size("head")
    seqs = lax.axis_size("seq")
    chunks = HEADS // group
    shard = tok * group
    seq = lax.axis_index("seq")
    first = (seq * group + lax.axis_index("head")) * tok
    ids = jnp.arange(widths.shape[0], dtype=jnp.int32)

    starts = jnp.sum((segment_ids[None, :] < ids[:, None]).astype(jnp.int32), axis=1)
    own = lax.dynamic_slice_in_dim(segment_ids, first, tok, 0)
    mine = own[None, :] == ids[:, None]
    own_start = jnp.sum(jnp.where(mine, starts[:, None], 0), axis=0)
    width = jnp.sum(jnp.where(mine, widths[:, None], 0), axis=0)
    offset = first + jnp.arange(tok, dtype=jnp.int32) - own_start
    row_pos = offset // width
    col_pos = offset - row_pos * width
    frequency = 10000.0 ** (-jnp.arange(QUARTER, dtype=jnp.float32) / QUARTER)
    places = jnp.stack([row_pos, col_pos]).astype(jnp.float32)
    angles = places[:, None, :] * frequency[None, :, None]
    turns = jnp.stack([jnp.cos(angles), jnp.sin(angles)], axis=1).reshape(4, QUARTER, tok)

    count = widths.shape[0]
    aug = -(-(HEAD + count + 1) // 128) * 128 - HEAD
    none = jnp.full((shard,), count, jnp.int32)
    padded = jnp.concatenate([none, segment_ids, none])
    key_seg = lax.dynamic_slice_in_dim(padded, seq * shard, 3 * shard, 0)
    lanes = jnp.arange(aug, dtype=jnp.int32)[None, :, None]
    key_seg = key_seg.reshape(3 * group, 1, tok)
    kaug = (key_seg == lanes).astype(jnp.bfloat16)
    query_seg = key_seg[group:2 * group]
    qaug = jnp.where((query_seg == lanes) | (lanes > count), 0.0, APART).astype(jnp.bfloat16)

    vmem = pl.BlockSpec(memory_space=pltpu.VMEM)
    dma = pltpu.SemaphoreType.DMA
    return pl.pallas_call(
        functools.partial(kernel, group, chunks, seqs),
        out_shape=jax.ShapeDtypeStruct((tok, D), jnp.bfloat16),
        in_specs=[vmem] * 4,
        out_specs=vmem,
        scratch_shapes=[
            pltpu.VMEM((chunks, group, 3, HEAD, tok), jnp.bfloat16),
            pltpu.VMEM((chunks, 3 * group, 3, HEAD, tok), jnp.bfloat16),
            pltpu.VMEM((3 * group, tok, HEAD + aug), jnp.bfloat16),
            pltpu.VMEM((chunks, group, HEAD, tok), jnp.bfloat16),
            pltpu.VMEM((chunks, group, HEAD, tok), jnp.bfloat16),
            dma((chunks, group - 1)),
            dma((chunks, group - 1)),
            dma((chunks,)),
            dma((chunks, 2)),
            dma((chunks, 2)),
            dma((chunks, group - 1)),
            dma((chunks, group - 1)),
            dma((chunks,)),
        ],
        compiler_params=pltpu.CompilerParams(
            collective_id=0, has_side_effects=True, vmem_limit_bytes=56 * 2**20
        ),
        cost_estimate=pl.CostEstimate(
            flops=4 * shard * shard * 2 * D // group, bytes_accessed=tok * D * 8, transcendentals=0
        ),
    )(projected, turns, kaug, qaug)


def solution(mesh):
    in_specs = (P(("seq", "head"), None), P(), P())
    out_specs = P(("seq", "head"), None)
    return jax.shard_map(body, mesh=mesh, in_specs=in_specs, out_specs=out_specs, check_vma=False)
```

```python
import functools
import math

import jax
import jax.numpy as jnp
from jax import lax
from jax.experimental import pallas as pl
from jax.experimental.pallas import tpu as pltpu
from jax.sharding import PartitionSpec as P

D = 2304
HEADS = 24
HEAD = D // HEADS
QUARTER = HEAD // 4
ONES = 16
APART = -131072.0
MESH = pl.DeviceIdType.MESH


def transposed(block):
    return jnp.transpose(block.astype(jnp.float32), (1, 0))


def kernel(
    group, chunks, seqs, count, x_ref, turns_ref, seg_ref, out_ref,
    send, held, keys, values, queries, blended, back,
    in_send, in_recv, in_own, halo_send, halo_recv, back_send, back_recv, back_own,
):
    tok = x_ref.shape[0]
    span = group * HEAD
    aug = queries.shape[0] - HEAD
    seq = lax.axis_index("seq")
    me = lax.axis_index("head")
    has_left = seq > 0
    has_right = seq < seqs - 1
    scale = math.log2(math.e) / math.sqrt(HEAD)

    barrier = pltpu.get_barrier_semaphore()
    for d in range(1, group):
        pl.semaphore_signal(
            barrier, inc=1, device_id={"head": lax.rem(me + d, group)}, device_id_type=MESH
        )

    @pl.when(has_left)
    def _():
        pl.semaphore_signal(barrier, inc=1, device_id={"seq": seq - 1}, device_id_type=MESH)

    @pl.when(has_right)
    def _():
        pl.semaphore_signal(barrier, inc=1, device_id={"seq": seq + 1}, device_id_type=MESH)

    pl.semaphore_wait(
        barrier, group - 1 + has_left.astype(jnp.int32) + has_right.astype(jnp.int32)
    )

    parts = ((0, 2), (2, 1))

    def in_copy(j, d, which):
        dest = lax.rem(me + d, group)
        first, size = parts[which]
        return pltpu.make_async_remote_copy(
            src_ref=send.at[j, dest, pl.ds(first, size)],
            dst_ref=held.at[j, group + me, pl.ds(first, size)],
            send_sem=in_send.at[j, d - 1, which],
            recv_sem=in_recv.at[j, d - 1, which],
            device_id={"head": dest},
            device_id_type=MESH,
        )

    def own_copy(j):
        return pltpu.make_async_copy(send.at[j, me], held.at[j, group + me], in_own.at[j])

    def halo_copy(j, side):
        slot = 0 if side == 0 else 2 * group
        return pltpu.make_async_remote_copy(
            src_ref=held.at[j, pl.ds(group, group), pl.ds(0, 2)],
            dst_ref=held.at[j, pl.ds(slot, group), pl.ds(0, 2)],
            send_sem=halo_send.at[j, side],
            recv_sem=halo_recv.at[j, side],
            device_id={"seq": seq + 1 if side == 0 else seq - 1},
            device_id_type=MESH,
        )

    def back_copy(j, d):
        dest = lax.rem(me + d, group)
        return pltpu.make_async_remote_copy(
            src_ref=blended.at[j, dest],
            dst_ref=back.at[j, me],
            send_sem=back_send.at[j, d - 1],
            recv_sem=back_recv.at[j, d - 1],
            device_id={"head": dest},
            device_id_type=MESH,
        )

    def back_own_copy(j):
        return pltpu.make_async_copy(blended.at[j, me], back.at[j, me], back_own.at[j])

    def prepare(j):
        for place, part in enumerate((1, 2, 0)):
            first = pl.multiple_of(part * D + j * span, 128)
            cols = transposed(x_ref[:, pl.ds(first, span)])
            for z in range(group):
                vals = cols[z * HEAD:(z + 1) * HEAD]
                if part < 2:
                    pieces = []
                    for half in range(2):
                        cosine, sine = turns_ref[2 * half], turns_ref[2 * half + 1]
                        low = vals[2 * half * QUARTER:(2 * half + 1) * QUARTER]
                        high = vals[(2 * half + 1) * QUARTER:(2 * half + 2) * QUARTER]
                        pieces += [low * cosine - high * sine, low * sine + high * cosine]
                    vals = jnp.concatenate(pieces, axis=0)
                send[j, z, place] = vals.astype(jnp.bfloat16)

    def issue(j, which):
        for d in range(1, group):
            in_copy(j, d, which).start()
        if which == 0:
            own_copy(j).start()

    def arrive(j, which):
        if which == 0:
            own_copy(j).wait()
        for d in range(1, group):
            in_copy(j, d, which).wait_recv()

    def halo_start(j):
        @pl.when(has_right)
        def _():
            halo_copy(j, 0).start()

        @pl.when(has_left)
        def _():
            halo_copy(j, 1).start()

    def halo_arrive(j):
        @pl.when(has_left)
        def _():
            halo_copy(j, 0).wait_recv()

        @pl.when(has_right)
        def _():
            halo_copy(j, 1).wait_recv()

        @pl.when(jnp.logical_not(has_left))
        def _():
            for z in range(group):
                held[j, z] = jnp.zeros((3, HEAD, tok), jnp.bfloat16)

        @pl.when(jnp.logical_not(has_right))
        def _():
            for z in range(group):
                held[j, 2 * group + z] = jnp.zeros((3, HEAD, tok), jnp.bfloat16)

    def back_start(j):
        for d in range(1, group):
            back_copy(j, d).start()
        back_own_copy(j).start()

    wide = 2 * tok
    lane = lax.broadcasted_iota(jnp.int32, (aug, tok), 0)

    def attend(j):
        for slot in range(3 * group):
            hot = jnp.where(seg_ref[slot] == lane, 1.0, 0.0)
            joined = jnp.concatenate([held[j, slot, 0].astype(jnp.float32), hot], axis=0)
            keys[pl.ds(slot * tok, tok)] = transposed(joined).astype(jnp.bfloat16)
            values[:HEAD, pl.ds(slot * tok, tok)] = held[j, slot, 1]
        for z in range(group):
            queries[:HEAD, pl.ds(z * tok, tok)] = held[j, group + z, 2]

        def query_block(i, carry):
            base = i * wide
            q = queries[:, pl.ds(pl.multiple_of(base, 128), wide)]

            def key_block(step, state):
                top, acc = state
                start = pl.multiple_of(base + step * wide, 128)
                s = jnp.dot(keys[pl.ds(start, wide)], q, preferred_element_type=jnp.float32)
                new_top = jnp.maximum(top, jnp.max(s, axis=0, keepdims=True))
                weights = jnp.exp2((s - new_top) * scale).astype(jnp.bfloat16)
                acc = acc * jnp.exp2((top - new_top) * scale) + jnp.dot(
                    values[:, pl.ds(start, wide)], weights, preferred_element_type=jnp.float32
                )
                return new_top, acc

            top = jnp.full((1, wide), -1e30, jnp.float32)
            acc = jnp.zeros((HEAD + ONES, wide), jnp.float32)
            top, acc = lax.fori_loop(0, group + 1, key_block, (top, acc))
            mean = (acc[:HEAD] / acc[HEAD:HEAD + 1]).astype(jnp.bfloat16)
            blended[j, 2 * i] = mean[:, :tok]
            blended[j, 2 * i + 1] = mean[:, tok:]
            return carry

        lax.fori_loop(0, group // 2, query_block, 0)

    prepare(0)
    issue(0, 0)
    issue(0, 1)
    prepare(1)
    values[HEAD:] = jnp.ones((ONES, values.shape[1]), jnp.bfloat16)
    for z in range(group):
        same = (seg_ref[group + z] == lane) | (lane > count)
        queries[HEAD:, pl.ds(z * tok, tok)] = jnp.where(same, 0.0, APART).astype(jnp.bfloat16)

    def step(t, carry):
        @pl.when(t < chunks)
        def _():
            arrive(t, 0)
            halo_start(t)

        @pl.when(t + 1 < chunks)
        def _():
            issue(t + 1, 0)

        @pl.when(t < chunks)
        def _():
            arrive(t, 1)

        @pl.when(t + 1 < chunks)
        def _():
            issue(t + 1, 1)

        @pl.when(t + 2 < chunks)
        def _():
            prepare(t + 2)

        @pl.when(t == chunks - 1)
        def _():
            for j in range(chunks - 2):
                back_start(j)

        @pl.when(t >= 1)
        def _():
            halo_arrive(t - 1)
            attend(t - 1)

        @pl.when(t >= chunks - 1)
        def _():
            back_start(t - 1)

        return carry

    lax.fori_loop(0, chunks + 1, step, 0)

    def finish(j, carry):
        back_own_copy(j).wait()
        for d in range(1, group):
            back_copy(j, d).wait_recv()
        rows = jnp.concatenate([back[j, z] for z in range(group)], axis=0)
        out_ref[:, pl.ds(pl.multiple_of(j * span, 128), span)] = transposed(rows).astype(
            jnp.bfloat16
        )
        for d in range(1, group):
            in_copy(j, d, 0).wait_send()
            in_copy(j, d, 1).wait_send()
            back_copy(j, d).wait_send()

        @pl.when(has_right)
        def _():
            halo_copy(j, 0).wait_send()

        @pl.when(has_left)
        def _():
            halo_copy(j, 1).wait_send()

        return carry

    lax.fori_loop(0, chunks, finish, 0)


def body(projected, segment_ids, widths):
    tok = projected.shape[0]
    group = lax.axis_size("head")
    seqs = lax.axis_size("seq")
    chunks = HEADS // group
    shard = tok * group
    seq = lax.axis_index("seq")
    first = (seq * group + lax.axis_index("head")) * tok
    ids = jnp.arange(widths.shape[0], dtype=jnp.int32)

    starts = jnp.sum((segment_ids[None, :] < ids[:, None]).astype(jnp.int32), axis=1)
    own = lax.dynamic_slice_in_dim(segment_ids, first, tok, 0)
    mine = own[None, :] == ids[:, None]
    own_start = jnp.sum(jnp.where(mine, starts[:, None], 0), axis=0)
    width = jnp.sum(jnp.where(mine, widths[:, None], 0), axis=0)
    offset = first + jnp.arange(tok, dtype=jnp.int32) - own_start
    row_pos = offset // width
    col_pos = offset - row_pos * width
    frequency = 10000.0 ** (-jnp.arange(QUARTER, dtype=jnp.float32) / QUARTER)
    places = jnp.stack([row_pos, col_pos]).astype(jnp.float32)
    angles = places[:, None, :] * frequency[None, :, None]
    turns = jnp.stack([jnp.cos(angles), jnp.sin(angles)], axis=1).reshape(4, QUARTER, tok)

    count = widths.shape[0]
    aug = -(-(HEAD + count + 1) // 128) * 128 - HEAD
    none = jnp.full((shard,), count, jnp.int32)
    padded = jnp.concatenate([none, segment_ids, none])
    key_seg = lax.dynamic_slice_in_dim(padded, seq * shard, 3 * shard, 0)
    key_seg = key_seg.reshape(3 * group, 1, tok)

    vmem = pl.BlockSpec(memory_space=pltpu.VMEM)
    dma = pltpu.SemaphoreType.DMA
    return pl.pallas_call(
        functools.partial(kernel, group, chunks, seqs, count),
        out_shape=jax.ShapeDtypeStruct((tok, D), jnp.bfloat16),
        in_specs=[vmem] * 3,
        out_specs=vmem,
        scratch_shapes=[
            pltpu.VMEM((chunks, group, 3, HEAD, tok), jnp.bfloat16),
            pltpu.VMEM((chunks, 3 * group, 3, HEAD, tok), jnp.bfloat16),
            pltpu.VMEM((3 * shard, HEAD + aug), jnp.bfloat16),
            pltpu.VMEM((HEAD + ONES, 3 * shard), jnp.bfloat16),
            pltpu.VMEM((HEAD + aug, shard), jnp.bfloat16),
            pltpu.VMEM((chunks, group, HEAD, tok), jnp.bfloat16),
            pltpu.VMEM((chunks, group, HEAD, tok), jnp.bfloat16),
            dma((chunks, group - 1, 2)),
            dma((chunks, group - 1, 2)),
            dma((chunks,)),
            dma((chunks, 2)),
            dma((chunks, 2)),
            dma((chunks, group - 1)),
            dma((chunks, group - 1)),
            dma((chunks,)),
        ],
        compiler_params=pltpu.CompilerParams(
            collective_id=0, has_side_effects=True, vmem_limit_bytes=56 * 2**20
        ),
        cost_estimate=pl.CostEstimate(
            flops=4 * shard * shard * 2 * D // group, bytes_accessed=tok * D * 8, transcendentals=0
        ),
    )(projected, turns, key_seg)


def solution(mesh):
    in_specs = (P(("seq", "head"), None), P(), P())
    out_specs = P(("seq", "head"), None)
    return jax.shard_map(body, mesh=mesh, in_specs=in_specs, out_specs=out_specs, check_vma=False)
```

```python
import functools
import math

import jax
import jax.numpy as jnp
from jax import lax
from jax.experimental import pallas as pl
from jax.experimental.pallas import tpu as pltpu
from jax.sharding import PartitionSpec as P

D = 2304
HEADS = 24
HEAD = D // HEADS
QUARTER = HEAD // 4
ONES = 16
APART = -131072.0
MESH = pl.DeviceIdType.MESH


def transposed(block):
    return jnp.transpose(block.astype(jnp.float32), (1, 0))


def kernel(
    group, chunks, seqs, count, x_ref, freq_ref, widths_ref, seg_ref, out_ref,
    x_held, turns, key_seg, send, held, keys, values, queries, blended, back,
    x_sem, in_send, in_recv, in_own, halo_send, halo_recv, back_send, back_recv, back_own,
):
    tok = x_ref.shape[0]
    blocks = seqs * group
    span = group * HEAD
    aug = queries.shape[0] - HEAD
    seq = lax.axis_index("seq")
    me = lax.axis_index("head")
    has_left = seq > 0
    has_right = seq < seqs - 1
    scale = math.log2(math.e) / math.sqrt(HEAD)

    columns = (2 * D, D, 0)

    def x_copy(j, part):
        first = pl.multiple_of(columns[part] + j * span, 128)
        return pltpu.make_async_copy(
            x_ref.at[:, pl.ds(first, span)], x_held.at[j, part], x_sem.at[j, part]
        )

    for j in range(chunks):
        for part in range(3):
            x_copy(j, part).start()

    barrier = pltpu.get_barrier_semaphore()
    for d in range(1, group):
        pl.semaphore_signal(
            barrier, inc=1, device_id={"head": lax.rem(me + d, group)}, device_id_type=MESH
        )

    @pl.when(has_left)
    def _():
        pl.semaphore_signal(barrier, inc=1, device_id={"seq": seq - 1}, device_id_type=MESH)

    @pl.when(has_right)
    def _():
        pl.semaphore_signal(barrier, inc=1, device_id={"seq": seq + 1}, device_id_type=MESH)

    pl.semaphore_wait(
        barrier, group - 1 + has_left.astype(jnp.int32) + has_right.astype(jnp.int32)
    )

    def in_copy(j, d, part):
        dest = lax.rem(me + d, group)
        return pltpu.make_async_remote_copy(
            src_ref=send.at[j, dest, part],
            dst_ref=held.at[j, group + me, part],
            send_sem=in_send.at[j, d - 1, part],
            recv_sem=in_recv.at[j, d - 1, part],
            device_id={"head": dest},
            device_id_type=MESH,
        )

    def own_copy(j, part):
        return pltpu.make_async_copy(
            send.at[j, me, part], held.at[j, group + me, part], in_own.at[j, part]
        )

    def halo_copy(j, side):
        slot = 0 if side == 0 else 2 * group
        return pltpu.make_async_remote_copy(
            src_ref=held.at[j, pl.ds(group, group), pl.ds(0, 2)],
            dst_ref=held.at[j, pl.ds(slot, group), pl.ds(0, 2)],
            send_sem=halo_send.at[j, side],
            recv_sem=halo_recv.at[j, side],
            device_id={"seq": seq + 1 if side == 0 else seq - 1},
            device_id_type=MESH,
        )

    def back_copy(j, d):
        dest = lax.rem(me + d, group)
        return pltpu.make_async_remote_copy(
            src_ref=blended.at[j, dest],
            dst_ref=back.at[j, me],
            send_sem=back_send.at[j, d - 1],
            recv_sem=back_recv.at[j, d - 1],
            device_id={"head": dest},
            device_id_type=MESH,
        )

    def back_own_copy(j):
        return pltpu.make_async_copy(blended.at[j, me], back.at[j, me], back_own.at[j])

    def prepare(j, part):
        x_copy(j, part).wait()
        cols = transposed(x_held[j, part])
        for z in range(group):
            vals = cols[z * HEAD:(z + 1) * HEAD]
            if part > 0:
                pieces = []
                for half in range(2):
                    cosine, sine = turns[2 * half], turns[2 * half + 1]
                    low = vals[2 * half * QUARTER:(2 * half + 1) * QUARTER]
                    high = vals[(2 * half + 1) * QUARTER:(2 * half + 2) * QUARTER]
                    pieces += [low * cosine - high * sine, low * sine + high * cosine]
                vals = jnp.concatenate(pieces, axis=0)
            send[j, z, part] = vals.astype(jnp.bfloat16)

    def issue(j, part):
        for d in range(1, group):
            in_copy(j, d, part).start()
        own_copy(j, part).start()

    def arrive(j, part):
        own_copy(j, part).wait()
        for d in range(1, group):
            in_copy(j, d, part).wait_recv()

    def lay_out():
        block = seq * group + me
        own = seg_ref[pl.ds(block, 1), :]
        everything = seg_ref[...]
        start = jnp.zeros((1, tok), jnp.int32)
        width = jnp.zeros((1, tok), jnp.int32)
        for sample in range(count):
            lower = jnp.sum(
                jnp.sum((everything < sample).astype(jnp.int32), axis=0, keepdims=True),
                axis=1, keepdims=True,
            )
            start = jnp.where(own == sample, lower, start)
            width = jnp.where(own == sample, widths_ref[sample], width)
        offset = block * tok + lax.broadcasted_iota(jnp.int32, (1, tok), 1) - start
        row = jnp.floor((offset.astype(jnp.float32) + 0.5) / width.astype(jnp.float32))
        col = offset.astype(jnp.float32) - row * width.astype(jnp.float32)
        for half, place in enumerate((row, col)):
            angles = freq_ref[...] * place
            turns[2 * half] = jnp.cos(angles)
            turns[2 * half + 1] = jnp.sin(angles)
        for slot in range(3 * group):
            number = (seq - 1) * group + slot
            ids = seg_ref[pl.ds(jnp.clip(number, 0, blocks - 1), 1), :]
            outside = jnp.logical_or(number < 0, number >= blocks).astype(jnp.int32)
            key_seg[slot] = ids * (1 - outside) + count * outside

    def halo_start(j):
        @pl.when(has_right)
        def _():
            halo_copy(j, 0).start()

        @pl.when(has_left)
        def _():
            halo_copy(j, 1).start()

    def halo_arrive(j):
        @pl.when(has_left)
        def _():
            halo_copy(j, 0).wait_recv()

        @pl.when(has_right)
        def _():
            halo_copy(j, 1).wait_recv()

        @pl.when(jnp.logical_not(has_left))
        def _():
            for z in range(group):
                held[j, z] = jnp.zeros((3, HEAD, tok), jnp.bfloat16)

        @pl.when(jnp.logical_not(has_right))
        def _():
            for z in range(group):
                held[j, 2 * group + z] = jnp.zeros((3, HEAD, tok), jnp.bfloat16)

    def back_start(j):
        for d in range(1, group):
            back_copy(j, d).start()
        back_own_copy(j).start()

    wide = 2 * tok
    lane = lax.broadcasted_iota(jnp.int32, (aug, tok), 0)

    def gather(j):
        for slot in range(3 * group):
            hot = jnp.where(key_seg[slot] == lane, 1.0, 0.0)
            joined = jnp.concatenate([held[j, slot, 1].astype(jnp.float32), hot], axis=0)
            keys[pl.ds(slot * tok, tok)] = transposed(joined).astype(jnp.bfloat16)
            values[:HEAD, pl.ds(slot * tok, tok)] = held[j, slot, 0]
        for z in range(group):
            queries[:HEAD, pl.ds(z * tok, tok)] = held[j, group + z, 2]

    def attend(j, first, last):
        def query_block(i, carry):
            base = i * wide
            q = queries[:, pl.ds(pl.multiple_of(base, 128), wide)]

            def key_block(step, state):
                top, acc = state
                start = pl.multiple_of(base + step * wide, 128)
                s = jnp.dot(keys[pl.ds(start, wide)], q, preferred_element_type=jnp.float32)
                new_top = jnp.maximum(top, jnp.max(s, axis=0, keepdims=True))
                weights = jnp.exp2((s - new_top) * scale).astype(jnp.bfloat16)
                acc = acc * jnp.exp2((top - new_top) * scale) + jnp.dot(
                    values[:, pl.ds(start, wide)], weights, preferred_element_type=jnp.float32
                )
                return new_top, acc

            top = jnp.full((1, wide), -1e30, jnp.float32)
            acc = jnp.zeros((HEAD + ONES, wide), jnp.float32)
            top, acc = lax.fori_loop(0, group + 1, key_block, (top, acc))
            mean = (acc[:HEAD] / acc[HEAD:HEAD + 1]).astype(jnp.bfloat16)
            blended[j, 2 * i] = mean[:, :tok]
            blended[j, 2 * i + 1] = mean[:, tok:]
            return carry

        lax.fori_loop(first, last, query_block, 0)

    prepare(0, 0)
    issue(0, 0)
    lay_out()
    for part in (1, 2):
        prepare(0, part)
        issue(0, part)
    for part in range(3):
        prepare(1, part)
    values[HEAD:] = jnp.ones((ONES, values.shape[1]), jnp.bfloat16)
    for z in range(group):
        same = (key_seg[group + z] == lane) | (lane > count)
        queries[HEAD:, pl.ds(z * tok, tok)] = jnp.where(same, 0.0, APART).astype(jnp.bfloat16)

    pairs = group // 2

    def step(t, carry):
        @pl.when(t >= 1)
        def _():
            halo_arrive(t - 1)
            gather(t - 1)
            attend(t - 1, 0, pairs // 2)

        @pl.when(t < chunks)
        def _():
            arrive(t, 0)
            arrive(t, 1)
            halo_start(t)

        @pl.when(t + 1 < chunks)
        def _():
            issue(t + 1, 0)
            issue(t + 1, 1)

        @pl.when(t >= 1)
        def _():
            attend(t - 1, pairs // 2, pairs)

        @pl.when(t < chunks)
        def _():
            arrive(t, 2)

        @pl.when(t + 1 < chunks)
        def _():
            issue(t + 1, 2)

        @pl.when(t == chunks - 1)
        def _():
            for j in range(chunks - 2):
                back_start(j)

        @pl.when(t >= chunks - 1)
        def _():
            back_start(t - 1)

        @pl.when(t + 2 < chunks)
        def _():
            for part in range(3):
                prepare(t + 2, part)

        return carry

    lax.fori_loop(0, chunks + 1, step, 0)

    def finish(j, carry):
        back_own_copy(j).wait()
        for d in range(1, group):
            back_copy(j, d).wait_recv()
        rows = jnp.concatenate([back[j, z] for z in range(group)], axis=0)
        out_ref[:, pl.ds(pl.multiple_of(j * span, 128), span)] = transposed(rows).astype(
            jnp.bfloat16
        )
        for d in range(1, group):
            for part in range(3):
                in_copy(j, d, part).wait_send()
            back_copy(j, d).wait_send()

        @pl.when(has_right)
        def _():
            halo_copy(j, 0).wait_send()

        @pl.when(has_left)
        def _():
            halo_copy(j, 1).wait_send()

        return carry

    lax.fori_loop(0, chunks, finish, 0)


def body(projected, segment_ids, widths):
    tok = projected.shape[0]
    group = lax.axis_size("head")
    seqs = lax.axis_size("seq")
    chunks = HEADS // group
    shard = tok * group
    count = widths.shape[0]
    aug = -(-(HEAD + count + 1) // 128) * 128 - HEAD
    frequency = 10000.0 ** (-jnp.arange(QUARTER, dtype=jnp.float32) / QUARTER)

    vmem = pl.BlockSpec(memory_space=pltpu.VMEM)
    dma = pltpu.SemaphoreType.DMA
    return pl.pallas_call(
        functools.partial(kernel, group, chunks, seqs, count),
        out_shape=jax.ShapeDtypeStruct((tok, D), jnp.bfloat16),
        in_specs=[
            pl.BlockSpec(memory_space=pl.ANY), vmem, pl.BlockSpec(memory_space=pltpu.SMEM), vmem
        ],
        out_specs=vmem,
        scratch_shapes=[
            pltpu.VMEM((chunks, 3, tok, group * HEAD), jnp.bfloat16),
            pltpu.VMEM((4, QUARTER, tok), jnp.float32),
            pltpu.VMEM((3 * group, 1, tok), jnp.int32),
            pltpu.VMEM((chunks, group, 3, HEAD, tok), jnp.bfloat16),
            pltpu.VMEM((chunks, 3 * group, 3, HEAD, tok), jnp.bfloat16),
            pltpu.VMEM((3 * shard, HEAD + aug), jnp.bfloat16),
            pltpu.VMEM((HEAD + ONES, 3 * shard), jnp.bfloat16),
            pltpu.VMEM((HEAD + aug, shard), jnp.bfloat16),
            pltpu.VMEM((chunks, group, HEAD, tok), jnp.bfloat16),
            pltpu.VMEM((chunks, group, HEAD, tok), jnp.bfloat16),
            dma((chunks, 3)),
            dma((chunks, group - 1, 3)),
            dma((chunks, group - 1, 3)),
            dma((chunks, 3)),
            dma((chunks, 2)),
            dma((chunks, 2)),
            dma((chunks, group - 1)),
            dma((chunks, group - 1)),
            dma((chunks,)),
        ],
        compiler_params=pltpu.CompilerParams(
            collective_id=0, has_side_effects=True, vmem_limit_bytes=56 * 2**20
        ),
        cost_estimate=pl.CostEstimate(
            flops=4 * shard * shard * 2 * D // group, bytes_accessed=tok * D * 8, transcendentals=0
        ),
    )(projected, frequency[:, None], widths, segment_ids.reshape(seqs * group, tok))


def solution(mesh):
    in_specs = (P(("seq", "head"), None), P(), P())
    out_specs = P(("seq", "head"), None)
    return jax.shard_map(body, mesh=mesh, in_specs=in_specs, out_specs=out_specs, check_vma=False)
```

```python
import functools
import math

import jax
import jax.numpy as jnp
import numpy as np
from jax import lax
from jax.experimental import pallas as pl
from jax.experimental.pallas import tpu as pltpu
from jax.sharding import PartitionSpec as P

D = 2304
HEADS = 24
HEAD = D // HEADS
QUARTER = HEAD // 4
ONES = 16
APART = -131072.0
MESH = pl.DeviceIdType.MESH


def transposed(block):
    return jnp.transpose(block, (1, 0))


def kernel(
    group, chunks, seqs, count, x_ref, freq_ref, widths_ref, seg_ref, out_ref,
    x_held, turns, key_seg, send, held, keys, values, queries, blended, back,
    x_sem, in_send, in_recv, in_own, halo_send, halo_recv, back_send, back_recv, back_own,
):
    tok = x_ref.shape[0]
    blocks = seqs * group
    span = group * HEAD
    aug = queries.shape[0] - HEAD
    seq = lax.axis_index("seq")
    me = lax.axis_index("head")
    has_left = seq > 0
    has_right = seq < seqs - 1
    scale = math.log2(math.e) / math.sqrt(HEAD)

    columns = (2 * D, D, 0)

    def x_copy(j, part):
        first = pl.multiple_of(columns[part] + j * span, 128)
        return pltpu.make_async_copy(
            x_ref.at[:, pl.ds(first, span)], x_held.at[j, part], x_sem.at[j, part]
        )

    for j in range(chunks):
        for part in range(3):
            x_copy(j, part).start()

    barrier = pltpu.get_barrier_semaphore()
    for d in range(1, group):
        pl.semaphore_signal(
            barrier, inc=1, device_id={"head": lax.rem(me + d, group)}, device_id_type=MESH
        )

    @pl.when(has_left)
    def _():
        pl.semaphore_signal(barrier, inc=1, device_id={"seq": seq - 1}, device_id_type=MESH)

    @pl.when(has_right)
    def _():
        pl.semaphore_signal(barrier, inc=1, device_id={"seq": seq + 1}, device_id_type=MESH)

    pl.semaphore_wait(
        barrier, group - 1 + has_left.astype(jnp.int32) + has_right.astype(jnp.int32)
    )

    def in_copy(j, d, part):
        dest = lax.rem(me + d, group)
        return pltpu.make_async_remote_copy(
            src_ref=send.at[j, dest, part],
            dst_ref=held.at[j, group + me, part],
            send_sem=in_send.at[j, d - 1, part],
            recv_sem=in_recv.at[j, d - 1, part],
            device_id={"head": dest},
            device_id_type=MESH,
        )

    def own_copy(j, part):
        return pltpu.make_async_copy(
            send.at[j, me, part], held.at[j, group + me, part], in_own.at[j, part]
        )

    def halo_copy(j, side):
        slot = 0 if side == 0 else 2 * group
        return pltpu.make_async_remote_copy(
            src_ref=held.at[j, pl.ds(group, group), pl.ds(0, 2)],
            dst_ref=held.at[j, pl.ds(slot, group), pl.ds(0, 2)],
            send_sem=halo_send.at[j, side],
            recv_sem=halo_recv.at[j, side],
            device_id={"seq": seq + 1 if side == 0 else seq - 1},
            device_id_type=MESH,
        )

    def back_copy(j, d):
        dest = lax.rem(me + d, group)
        return pltpu.make_async_remote_copy(
            src_ref=blended.at[j, dest],
            dst_ref=back.at[j, me],
            send_sem=back_send.at[j, d - 1],
            recv_sem=back_recv.at[j, d - 1],
            device_id={"head": dest},
            device_id_type=MESH,
        )

    def back_own_copy(j):
        return pltpu.make_async_copy(blended.at[j, me], back.at[j, me], back_own.at[j])

    def prepare(j, part):
        x_copy(j, part).wait()
        cols = transposed(x_held[j, part])
        for z in range(group):
            vals = cols[z * HEAD:(z + 1) * HEAD]
            if part > 0:
                vals = vals.astype(jnp.float32)
                pieces = []
                for half in range(2):
                    cosine, sine = turns[2 * half], turns[2 * half + 1]
                    low = vals[2 * half * QUARTER:(2 * half + 1) * QUARTER]
                    high = vals[(2 * half + 1) * QUARTER:(2 * half + 2) * QUARTER]
                    pieces += [low * cosine - high * sine, low * sine + high * cosine]
                vals = jnp.concatenate(pieces, axis=0)
            send[j, z, part] = vals.astype(jnp.bfloat16)

    def issue(j, part):
        for d in range(1, group):
            in_copy(j, d, part).start()
        own_copy(j, part).start()

    def arrive(j, part):
        own_copy(j, part).wait()
        for d in range(1, group):
            in_copy(j, d, part).wait_recv()

    rows = tok // seg_ref.shape[1]

    def ids_of(block):
        pieces = [seg_ref[pl.ds(block * rows + r, 1), :] for r in range(rows)]
        return jnp.concatenate(pieces, axis=1)

    def lay_out():
        block = seq * group + me
        own = ids_of(block)
        everything = seg_ref[...]
        start = jnp.zeros((1, tok), jnp.int32)
        width = jnp.zeros((1, tok), jnp.int32)
        for sample in range(count):
            lower = jnp.sum(
                jnp.sum((everything < sample).astype(jnp.int32), axis=0, keepdims=True),
                axis=1, keepdims=True,
            )
            start = jnp.where(own == sample, lower, start)
            width = jnp.where(own == sample, widths_ref[sample], width)
        offset = block * tok + lax.broadcasted_iota(jnp.int32, (1, tok), 1) - start
        row = jnp.floor((offset.astype(jnp.float32) + 0.5) / width.astype(jnp.float32))
        col = offset.astype(jnp.float32) - row * width.astype(jnp.float32)
        for half, place in enumerate((row, col)):
            angles = freq_ref[...] * place
            turns[2 * half] = jnp.cos(angles)
            turns[2 * half + 1] = jnp.sin(angles)
        for slot in range(3 * group):
            number = (seq - 1) * group + slot
            ids = ids_of(jnp.clip(number, 0, blocks - 1))
            outside = jnp.logical_or(number < 0, number >= blocks).astype(jnp.int32)
            key_seg[slot] = ids * (1 - outside) + count * outside

    def halo_start(j):
        @pl.when(has_right)
        def _():
            halo_copy(j, 0).start()

        @pl.when(has_left)
        def _():
            halo_copy(j, 1).start()

    def halo_arrive(j):
        @pl.when(has_left)
        def _():
            halo_copy(j, 0).wait_recv()

        @pl.when(has_right)
        def _():
            halo_copy(j, 1).wait_recv()

        @pl.when(jnp.logical_not(has_left))
        def _():
            for z in range(group):
                held[j, z] = jnp.zeros((3, HEAD, tok), jnp.bfloat16)

        @pl.when(jnp.logical_not(has_right))
        def _():
            for z in range(group):
                held[j, 2 * group + z] = jnp.zeros((3, HEAD, tok), jnp.bfloat16)

    def back_start(j, first=0, last=group):
        for d in range(1, group):
            dest = lax.rem(me + d, group)

            @pl.when(jnp.logical_and(dest >= first, dest < last))
            def _():
                back_copy(j, d).start()

        @pl.when(jnp.logical_and(me >= first, me < last))
        def _():
            back_own_copy(j).start()

    wide = 2 * tok
    lane = lax.broadcasted_iota(jnp.int32, (aug, tok), 0)

    def gather(j):
        for slot in range(3 * group):
            hot = jnp.where(key_seg[slot] == lane, 1.0, 0.0).astype(jnp.bfloat16)
            joined = jnp.concatenate([held[j, slot, 1], hot], axis=0)
            keys[pl.ds(slot * tok, tok)] = transposed(joined)
            values[:HEAD, pl.ds(slot * tok, tok)] = held[j, slot, 0]
        for z in range(group):
            queries[:HEAD, pl.ds(z * tok, tok)] = held[j, group + z, 2]

    def attend(j, first, last):
        def query_block(i, carry):
            base = i * wide
            q = queries[:, pl.ds(pl.multiple_of(base, 128), wide)]

            def key_block(step, state):
                top, acc = state
                start = pl.multiple_of(base + step * wide, 128)
                s = jnp.dot(keys[pl.ds(start, wide)], q, preferred_element_type=jnp.float32)
                new_top = jnp.maximum(top, jnp.max(s, axis=0, keepdims=True))
                weights = jnp.exp2((s - new_top) * scale).astype(jnp.bfloat16)
                acc = acc * jnp.exp2((top - new_top) * scale) + jnp.dot(
                    values[:, pl.ds(start, wide)], weights, preferred_element_type=jnp.float32
                )
                return new_top, acc

            top = jnp.full((1, wide), -1e30, jnp.float32)
            acc = jnp.zeros((HEAD + ONES, wide), jnp.float32)
            top, acc = lax.fori_loop(0, group + 1, key_block, (top, acc))
            mean = (acc[:HEAD] / acc[HEAD:HEAD + 1]).astype(jnp.bfloat16)
            blended[j, 2 * i] = mean[:, :tok]
            blended[j, 2 * i + 1] = mean[:, tok:]
            return carry

        lax.fori_loop(first, last, query_block, 0)

    prepare(0, 0)
    issue(0, 0)
    lay_out()
    for part in (1, 2):
        prepare(0, part)
        issue(0, part)
    for part in range(3):
        prepare(1, part)
    values[HEAD:] = jnp.ones((ONES, values.shape[1]), jnp.bfloat16)
    for z in range(group):
        same = (key_seg[group + z] == lane) | (lane > count)
        queries[HEAD:, pl.ds(z * tok, tok)] = jnp.where(same, 0.0, APART).astype(jnp.bfloat16)

    pairs = group // 2

    def step(t, carry):
        @pl.when(t >= 1)
        def _():
            halo_arrive(t - 1)
            gather(t - 1)
            attend(t - 1, 0, pairs // 2)

        @pl.when(t == chunks)
        def _():
            back_start(t - 1, 0, pairs // 2 * 2)

        @pl.when(t < chunks)
        def _():
            arrive(t, 0)
            arrive(t, 1)
            halo_start(t)

        @pl.when(t + 1 < chunks)
        def _():
            for part in range(3):
                issue(t + 1, part)

        @pl.when(t == chunks - 1)
        def _():
            for j in range(chunks - 2):
                back_start(j)

        @pl.when(t >= 1)
        def _():
            attend(t - 1, pairs // 2, pairs)

        @pl.when(t < chunks)
        def _():
            arrive(t, 2)

        @pl.when(t == chunks - 1)
        def _():
            back_start(t - 1)

        @pl.when(t == chunks)
        def _():
            back_start(t - 1, pairs // 2 * 2, group)

        @pl.when(t + 2 < chunks)
        def _():
            for part in range(3):
                prepare(t + 2, part)

        return carry

    lax.fori_loop(0, chunks + 1, step, 0)

    def finish(j, carry):
        back_own_copy(j).wait()
        for d in range(1, group):
            back_copy(j, d).wait_recv()
        rows = jnp.concatenate([back[j, z] for z in range(group)], axis=0)
        out_ref[:, pl.ds(pl.multiple_of(j * span, 128), span)] = transposed(rows)
        for d in range(1, group):
            for part in range(3):
                in_copy(j, d, part).wait_send()
            back_copy(j, d).wait_send()

        @pl.when(has_right)
        def _():
            halo_copy(j, 0).wait_send()

        @pl.when(has_left)
        def _():
            halo_copy(j, 1).wait_send()

        return carry

    lax.fori_loop(0, chunks, finish, 0)


def body(projected, segment_ids, widths):
    tok = projected.shape[0]
    group = lax.axis_size("head")
    seqs = lax.axis_size("seq")
    chunks = HEADS // group
    shard = tok * group
    count = widths.shape[0]
    aug = -(-(HEAD + count + 1) // 128) * 128 - HEAD
    frequency = 10000.0 ** (-np.arange(QUARTER, dtype=np.float64) / QUARTER)
    frequency = jnp.asarray(frequency.astype(np.float32))

    vmem = pl.BlockSpec(memory_space=pltpu.VMEM)
    dma = pltpu.SemaphoreType.DMA
    return pl.pallas_call(
        functools.partial(kernel, group, chunks, seqs, count),
        out_shape=jax.ShapeDtypeStruct((tok, D), jnp.bfloat16),
        in_specs=[
            pl.BlockSpec(memory_space=pl.ANY), vmem, pl.BlockSpec(memory_space=pltpu.SMEM), vmem
        ],
        out_specs=vmem,
        scratch_shapes=[
            pltpu.VMEM((chunks, 3, tok, group * HEAD), jnp.bfloat16),
            pltpu.VMEM((4, QUARTER, tok), jnp.float32),
            pltpu.VMEM((3 * group, 1, tok), jnp.int32),
            pltpu.VMEM((chunks, group, 3, HEAD, tok), jnp.bfloat16),
            pltpu.VMEM((chunks, 3 * group, 3, HEAD, tok), jnp.bfloat16),
            pltpu.VMEM((3 * shard, HEAD + aug), jnp.bfloat16),
            pltpu.VMEM((HEAD + ONES, 3 * shard), jnp.bfloat16),
            pltpu.VMEM((HEAD + aug, shard), jnp.bfloat16),
            pltpu.VMEM((chunks, group, HEAD, tok), jnp.bfloat16),
            pltpu.VMEM((chunks, group, HEAD, tok), jnp.bfloat16),
            dma((chunks, 3)),
            dma((chunks, group - 1, 3)),
            dma((chunks, group - 1, 3)),
            dma((chunks, 3)),
            dma((chunks, 2)),
            dma((chunks, 2)),
            dma((chunks, group - 1)),
            dma((chunks, group - 1)),
            dma((chunks,)),
        ],
        compiler_params=pltpu.CompilerParams(
            collective_id=0, has_side_effects=True, vmem_limit_bytes=56 * 2**20
        ),
        cost_estimate=pl.CostEstimate(
            flops=4 * shard * shard * 2 * D // group, bytes_accessed=tok * D * 8, transcendentals=0
        ),
    )(projected, frequency[:, None], widths, segment_ids.reshape(-1, 128 if tok % 128 == 0 else tok))


def solution(mesh):
    in_specs = (P(("seq", "head"), None), P(), P())
    out_specs = P(("seq", "head"), None)
    return jax.shard_map(body, mesh=mesh, in_specs=in_specs, out_specs=out_specs, check_vma=False)
```

```python
import functools
import math

import jax
import jax.numpy as jnp
import numpy as np
from jax import lax
from jax.experimental import pallas as pl
from jax.experimental.pallas import tpu as pltpu
from jax.sharding import PartitionSpec as P

D = 2304
HEADS = 24
HEAD = D // HEADS
QUARTER = HEAD // 4
ONES = 16
APART = -131072.0
MESH = pl.DeviceIdType.MESH


def transposed(block):
    return jnp.transpose(block, (1, 0))


def kernel(
    group, chunks, seqs, count, x_ref, freq_ref, widths_ref, seg_ref, back,
    x_held, turns, key_seg, send, held, keys, values, queries, blended,
    x_sem, in_send, in_recv, in_own, halo_send, halo_recv, back_send, back_recv, back_own,
):
    tok = x_ref.shape[0]
    blocks = seqs * group
    span = group * HEAD
    aug = queries.shape[0] - HEAD
    seq = lax.axis_index("seq")
    me = lax.axis_index("head")
    has_left = seq > 0
    has_right = seq < seqs - 1
    scale = math.log2(math.e) / math.sqrt(HEAD)

    def partner(d):
        place, found = 1, 0
        while place < group:
            found = found + lax.rem(me // place + d // place, 2) * place
            place *= 2
        return found

    partners = range(group - 1, 0, -1)

    columns = (2 * D, D, 0)

    def x_copy(j, part):
        first = pl.multiple_of(columns[part] + j * span, 128)
        return pltpu.make_async_copy(
            x_ref.at[:, pl.ds(first, span)], x_held.at[j, part], x_sem.at[j, part]
        )

    for part in range(3):
        x_copy(0, part).start()

    barrier = pltpu.get_barrier_semaphore()
    for d in partners:
        pl.semaphore_signal(
            barrier, inc=1, device_id={"head": partner(d)}, device_id_type=MESH
        )

    @pl.when(has_left)
    def _():
        pl.semaphore_signal(barrier, inc=1, device_id={"seq": seq - 1}, device_id_type=MESH)

    @pl.when(has_right)
    def _():
        pl.semaphore_signal(barrier, inc=1, device_id={"seq": seq + 1}, device_id_type=MESH)

    pl.semaphore_wait(
        barrier, group - 1 + has_left.astype(jnp.int32) + has_right.astype(jnp.int32)
    )

    def in_copy(j, d, part):
        dest = partner(d)
        return pltpu.make_async_remote_copy(
            src_ref=send.at[j, dest, part],
            dst_ref=held.at[j, group + me, part],
            send_sem=in_send.at[j, d - 1, part],
            recv_sem=in_recv.at[j, d - 1, part],
            device_id={"head": dest},
            device_id_type=MESH,
        )

    def own_copy(j, part):
        return pltpu.make_async_copy(
            send.at[j, me, part], held.at[j, group + me, part], in_own.at[j, part]
        )

    def halo_copy(j, side):
        slot = 0 if side == 0 else 2 * group
        return pltpu.make_async_remote_copy(
            src_ref=held.at[j, pl.ds(group, group), pl.ds(0, 2)],
            dst_ref=held.at[j, pl.ds(slot, group), pl.ds(0, 2)],
            send_sem=halo_send.at[j, side],
            recv_sem=halo_recv.at[j, side],
            device_id={"seq": seq + 1 if side == 0 else seq - 1},
            device_id_type=MESH,
        )

    def back_copy(j, d):
        dest = partner(d)
        return pltpu.make_async_remote_copy(
            src_ref=blended.at[j, dest],
            dst_ref=back.at[j, me],
            send_sem=back_send.at[j, d - 1],
            recv_sem=back_recv.at[j, d - 1],
            device_id={"head": dest},
            device_id_type=MESH,
        )

    def back_own_copy(j):
        return pltpu.make_async_copy(blended.at[j, me], back.at[j, me], back_own.at[j])

    def prepare(j, part):
        x_copy(j, part).wait()
        cols = transposed(x_held[j, part])
        for z in range(group):
            vals = cols[z * HEAD:(z + 1) * HEAD]
            if part > 0:
                vals = vals.astype(jnp.float32)
                pieces = []
                for half in range(2):
                    cosine, sine = turns[2 * half], turns[2 * half + 1]
                    low = vals[2 * half * QUARTER:(2 * half + 1) * QUARTER]
                    high = vals[(2 * half + 1) * QUARTER:(2 * half + 2) * QUARTER]
                    pieces += [low * cosine - high * sine, low * sine + high * cosine]
                vals = jnp.concatenate(pieces, axis=0)
            send[j, z, part] = vals.astype(jnp.bfloat16)

    def issue(j, part):
        for d in partners:
            in_copy(j, d, part).start()
        own_copy(j, part).start()

    def arrive(j, part):
        own_copy(j, part).wait()
        for d in partners:
            in_copy(j, d, part).wait_recv()

    rows = tok // seg_ref.shape[1]

    def ids_of(block):
        pieces = [seg_ref[pl.ds(block * rows + r, 1), :] for r in range(rows)]
        return jnp.concatenate(pieces, axis=1)

    def lay_out():
        block = seq * group + me
        own = ids_of(block)
        everything = seg_ref[...]
        start = jnp.zeros((1, tok), jnp.int32)
        width = jnp.zeros((1, tok), jnp.int32)
        for sample in range(count):
            lower = jnp.sum(
                jnp.sum((everything < sample).astype(jnp.int32), axis=0, keepdims=True),
                axis=1, keepdims=True,
            )
            start = jnp.where(own == sample, lower, start)
            width = jnp.where(own == sample, widths_ref[sample], width)
        offset = block * tok + lax.broadcasted_iota(jnp.int32, (1, tok), 1) - start
        row = jnp.floor((offset.astype(jnp.float32) + 0.5) / width.astype(jnp.float32))
        col = offset.astype(jnp.float32) - row * width.astype(jnp.float32)
        for half, place in enumerate((row, col)):
            angles = freq_ref[...] * place
            turns[2 * half] = jnp.cos(angles)
            turns[2 * half + 1] = jnp.sin(angles)
        for slot in range(3 * group):
            number = (seq - 1) * group + slot
            ids = ids_of(jnp.clip(number, 0, blocks - 1))
            outside = jnp.logical_or(number < 0, number >= blocks).astype(jnp.int32)
            key_seg[slot] = ids * (1 - outside) + count * outside

    def halo_start(j):
        @pl.when(has_right)
        def _():
            halo_copy(j, 0).start()

        @pl.when(has_left)
        def _():
            halo_copy(j, 1).start()

    def halo_arrive(j):
        @pl.when(has_left)
        def _():
            halo_copy(j, 0).wait_recv()

        @pl.when(has_right)
        def _():
            halo_copy(j, 1).wait_recv()

        @pl.when(jnp.logical_not(has_left))
        def _():
            for z in range(group):
                held[j, z] = jnp.zeros((3, HEAD, tok), jnp.bfloat16)

        @pl.when(jnp.logical_not(has_right))
        def _():
            for z in range(group):
                held[j, 2 * group + z] = jnp.zeros((3, HEAD, tok), jnp.bfloat16)

    def back_start(j, first=0, last=group):
        for d in partners:
            dest = partner(d)

            @pl.when(jnp.logical_and(dest >= first, dest < last))
            def _():
                back_copy(j, d).start()

        @pl.when(jnp.logical_and(me >= first, me < last))
        def _():
            back_own_copy(j).start()

    wide = 2 * tok
    lane = lax.broadcasted_iota(jnp.int32, (aug, tok), 0)

    def gather(j):
        for slot in range(3 * group):
            hot = jnp.where(key_seg[slot] == lane, 1.0, 0.0).astype(jnp.bfloat16)
            joined = jnp.concatenate([held[j, slot, 1], hot], axis=0)
            keys[pl.ds(slot * tok, tok)] = transposed(joined)
            values[:HEAD, pl.ds(slot * tok, tok)] = held[j, slot, 0]
        for z in range(group):
            queries[:HEAD, pl.ds(z * tok, tok)] = held[j, group + z, 2]

    def attend(j, first, last):
        def query_block(i, carry):
            base = i * wide
            q = queries[:, pl.ds(pl.multiple_of(base, 128), wide)]

            def key_block(step, state):
                top, acc = state
                start = pl.multiple_of(base + step * wide, 128)
                s = jnp.dot(keys[pl.ds(start, wide)], q, preferred_element_type=jnp.float32)
                new_top = jnp.maximum(top, jnp.max(s, axis=0, keepdims=True))
                weights = jnp.exp2((s - new_top) * scale).astype(jnp.bfloat16)
                acc = acc * jnp.exp2((top - new_top) * scale) + jnp.dot(
                    values[:, pl.ds(start, wide)], weights, preferred_element_type=jnp.float32
                )
                return new_top, acc

            top = jnp.full((1, wide), -1e30, jnp.float32)
            acc = jnp.zeros((HEAD + ONES, wide), jnp.float32)
            top, acc = lax.fori_loop(0, group + 1, key_block, (top, acc))
            mean = (acc[:HEAD] / acc[HEAD:HEAD + 1]).astype(jnp.bfloat16)
            blended[j, 2 * i] = mean[:, :tok]
            blended[j, 2 * i + 1] = mean[:, tok:]
            return carry

        lax.fori_loop(first, last, query_block, 0)

    prepare(0, 0)
    issue(0, 0)
    for j in range(1, chunks):
        for part in range(3):
            x_copy(j, part).start()
    lay_out()
    for part in (1, 2):
        prepare(0, part)
        issue(0, part)
    for part in range(3):
        prepare(1, part)
    values[HEAD:] = jnp.ones((ONES, values.shape[1]), jnp.bfloat16)
    for z in range(group):
        same = (key_seg[group + z] == lane) | (lane > count)
        queries[HEAD:, pl.ds(z * tok, tok)] = jnp.where(same, 0.0, APART).astype(jnp.bfloat16)

    pairs = group // 2

    def step(t, carry):
        @pl.when(t >= 1)
        def _():
            halo_arrive(t - 1)
            gather(t - 1)
            attend(t - 1, 0, pairs // 2)

        @pl.when(t == chunks)
        def _():
            back_start(t - 1, 0, pairs // 2 * 2)

        @pl.when(t < chunks)
        def _():
            arrive(t, 0)
            arrive(t, 1)
            halo_start(t)

        @pl.when(t + 1 < chunks)
        def _():
            for part in range(3):
                issue(t + 1, part)

        @pl.when(t == chunks - 1)
        def _():
            for j in range(chunks - 2):
                back_start(j)

        @pl.when(t >= 1)
        def _():
            attend(t - 1, pairs // 2, pairs)

        @pl.when(t < chunks)
        def _():
            arrive(t, 2)

        @pl.when(t == chunks - 1)
        def _():
            back_start(t - 1)

        @pl.when(t == chunks)
        def _():
            back_start(t - 1, pairs // 2 * 2, group)

        @pl.when(t + 2 < chunks)
        def _():
            for part in range(3):
                prepare(t + 2, part)

        return carry

    lax.fori_loop(0, chunks + 1, step, 0)

    def finish(j, carry):
        back_own_copy(j).wait()
        for d in partners:
            back_copy(j, d).wait_recv()
        for d in partners:
            for part in range(3):
                in_copy(j, d, part).wait_send()
            back_copy(j, d).wait_send()

        @pl.when(has_right)
        def _():
            halo_copy(j, 0).wait_send()

        @pl.when(has_left)
        def _():
            halo_copy(j, 1).wait_send()

        return carry

    lax.fori_loop(0, chunks, finish, 0)


def turned(back_ref, out_ref):
    rows = jnp.concatenate([back_ref[0, z] for z in range(back_ref.shape[1])], axis=0)
    out_ref[...] = transposed(rows)


def body(projected, segment_ids, widths):
    tok = projected.shape[0]
    group = lax.axis_size("head")
    seqs = lax.axis_size("seq")
    chunks = HEADS // group
    shard = tok * group
    count = widths.shape[0]
    aug = -(-(HEAD + count + 1) // 128) * 128 - HEAD
    frequency = 10000.0 ** (-np.arange(QUARTER, dtype=np.float64) / QUARTER)
    frequency = jnp.asarray(frequency.astype(np.float32))

    vmem = pl.BlockSpec(memory_space=pltpu.VMEM)
    dma = pltpu.SemaphoreType.DMA
    back = pl.pallas_call(
        functools.partial(kernel, group, chunks, seqs, count),
        out_shape=jax.ShapeDtypeStruct((chunks, group, HEAD, tok), jnp.bfloat16),
        in_specs=[
            pl.BlockSpec(memory_space=pl.ANY), vmem, pl.BlockSpec(memory_space=pltpu.SMEM), vmem
        ],
        out_specs=pl.BlockSpec(memory_space=pl.ANY),
        scratch_shapes=[
            pltpu.VMEM((chunks, 3, tok, group * HEAD), jnp.bfloat16),
            pltpu.VMEM((4, QUARTER, tok), jnp.float32),
            pltpu.VMEM((3 * group, 1, tok), jnp.int32),
            pltpu.VMEM((chunks, group, 3, HEAD, tok), jnp.bfloat16),
            pltpu.VMEM((chunks, 3 * group, 3, HEAD, tok), jnp.bfloat16),
            pltpu.VMEM((3 * shard, HEAD + aug), jnp.bfloat16),
            pltpu.VMEM((HEAD + ONES, 3 * shard), jnp.bfloat16),
            pltpu.VMEM((HEAD + aug, shard), jnp.bfloat16),
            pltpu.VMEM((chunks, group, HEAD, tok), jnp.bfloat16),
            dma((chunks, 3)),
            dma((chunks, group - 1, 3)),
            dma((chunks, group - 1, 3)),
            dma((chunks, 3)),
            dma((chunks, 2)),
            dma((chunks, 2)),
            dma((chunks, group - 1)),
            dma((chunks, group - 1)),
            dma((chunks,)),
        ],
        compiler_params=pltpu.CompilerParams(
            collective_id=0, has_side_effects=True, vmem_limit_bytes=56 * 2**20
        ),
        cost_estimate=pl.CostEstimate(
            flops=4 * shard * shard * 2 * D // group, bytes_accessed=tok * D * 8, transcendentals=0
        ),
    )(projected, frequency[:, None], widths, segment_ids.reshape(-1, 128 if tok % 128 == 0 else tok))
    return pl.pallas_call(
        turned,
        grid=(chunks,),
        out_shape=jax.ShapeDtypeStruct((tok, D), jnp.bfloat16),
        in_specs=[pl.BlockSpec((1, group, HEAD, tok), lambda j: (j, 0, 0, 0))],
        out_specs=pl.BlockSpec((tok, group * HEAD), lambda j: (0, j)),
    )(back)


def solution(mesh):
    in_specs = (P(("seq", "head"), None), P(), P())
    out_specs = P(("seq", "head"), None)
    return jax.shard_map(body, mesh=mesh, in_specs=in_specs, out_specs=out_specs, check_vma=False)
```

```python
import functools
import math

import jax
import jax.numpy as jnp
import numpy as np
from jax import lax
from jax.experimental import pallas as pl
from jax.experimental.pallas import tpu as pltpu
from jax.sharding import PartitionSpec as P

D = 2304
HEADS = 24
HEAD = D // HEADS
QUARTER = HEAD // 4
ONES = 16
APART = -131072.0
MESH = pl.DeviceIdType.MESH


def transposed(block):
    return jnp.transpose(block, (1, 0))


def kernel(
    group, chunks, seqs, count, x_ref, freq_ref, widths_ref, seg_ref, out_ref,
    x_held, turns, key_seg, send, held, keys, values, queries, blended, back,
    x_sem, in_send, in_recv, in_own, halo_send, halo_recv, back_send, back_recv, back_own,
):
    tok = x_ref.shape[0]
    blocks = seqs * group
    span = group * HEAD
    aug = queries.shape[0] - HEAD
    seq = lax.axis_index("seq")
    me = lax.axis_index("head")
    has_left = seq > 0
    has_right = seq < seqs - 1
    scale = math.log2(math.e) / math.sqrt(HEAD)

    def partner(d):
        place, found = 1, 0
        while place < group:
            found = found + lax.rem(me // place + d // place, 2) * place
            place *= 2
        return found

    partners = range(group - 1, 0, -1)

    columns = (2 * D, D, 0)

    def x_copy(j, part):
        first = pl.multiple_of(columns[part] + j * span, 128)
        return pltpu.make_async_copy(
            x_ref.at[:, pl.ds(first, span)], x_held.at[j, part], x_sem.at[j, part]
        )

    for part in range(3):
        x_copy(0, part).start()

    barrier = pltpu.get_barrier_semaphore()
    for d in partners:
        pl.semaphore_signal(
            barrier, inc=1, device_id={"head": partner(d)}, device_id_type=MESH
        )

    @pl.when(has_left)
    def _():
        pl.semaphore_signal(barrier, inc=1, device_id={"seq": seq - 1}, device_id_type=MESH)

    @pl.when(has_right)
    def _():
        pl.semaphore_signal(barrier, inc=1, device_id={"seq": seq + 1}, device_id_type=MESH)

    pl.semaphore_wait(
        barrier, group - 1 + has_left.astype(jnp.int32) + has_right.astype(jnp.int32)
    )

    def in_copy(j, d, part):
        dest = partner(d)
        return pltpu.make_async_remote_copy(
            src_ref=send.at[j, dest, part],
            dst_ref=held.at[j, group + me, part],
            send_sem=in_send.at[j, d - 1, part],
            recv_sem=in_recv.at[j, d - 1, part],
            device_id={"head": dest},
            device_id_type=MESH,
        )

    def own_copy(j, part):
        return pltpu.make_async_copy(
            send.at[j, me, part], held.at[j, group + me, part], in_own.at[j, part]
        )

    def halo_copy(j, side):
        slot = 0 if side == 0 else 2 * group
        return pltpu.make_async_remote_copy(
            src_ref=held.at[j, pl.ds(group, group), pl.ds(0, 2)],
            dst_ref=held.at[j, pl.ds(slot, group), pl.ds(0, 2)],
            send_sem=halo_send.at[j, side],
            recv_sem=halo_recv.at[j, side],
            device_id={"seq": seq + 1 if side == 0 else seq - 1},
            device_id_type=MESH,
        )

    def back_copy(j, d):
        dest = partner(d)
        return pltpu.make_async_remote_copy(
            src_ref=blended.at[j, dest],
            dst_ref=back.at[j, me],
            send_sem=back_send.at[j, d - 1],
            recv_sem=back_recv.at[j, d - 1],
            device_id={"head": dest},
            device_id_type=MESH,
        )

    def back_own_copy(j):
        return pltpu.make_async_copy(blended.at[j, me], back.at[j, me], back_own.at[j])

    def prepare(j, part):
        x_copy(j, part).wait()
        cols = transposed(x_held[j, part])
        for z in range(group):
            vals = cols[z * HEAD:(z + 1) * HEAD]
            if part > 0:
                vals = vals.astype(jnp.float32)
                pieces = []
                for half in range(2):
                    cosine, sine = turns[2 * half], turns[2 * half + 1]
                    low = vals[2 * half * QUARTER:(2 * half + 1) * QUARTER]
                    high = vals[(2 * half + 1) * QUARTER:(2 * half + 2) * QUARTER]
                    pieces += [low * cosine - high * sine, low * sine + high * cosine]
                vals = jnp.concatenate(pieces, axis=0)
            send[j, z, part] = vals.astype(jnp.bfloat16)

    def issue(j, part):
        for d in partners:
            in_copy(j, d, part).start()
        own_copy(j, part).start()

    def arrive(j, part):
        own_copy(j, part).wait()
        for d in partners:
            in_copy(j, d, part).wait_recv()

    rows = tok // seg_ref.shape[1]

    def ids_of(block):
        pieces = [seg_ref[pl.ds(block * rows + r, 1), :] for r in range(rows)]
        return jnp.concatenate(pieces, axis=1)

    def lay_out():
        block = seq * group + me
        own = ids_of(block)
        everything = seg_ref[...]
        start = jnp.zeros((1, tok), jnp.int32)
        width = jnp.zeros((1, tok), jnp.int32)
        for sample in range(count):
            lower = jnp.sum(
                jnp.sum((everything < sample).astype(jnp.int32), axis=0, keepdims=True),
                axis=1, keepdims=True,
            )
            start = jnp.where(own == sample, lower, start)
            width = jnp.where(own == sample, widths_ref[sample], width)
        offset = block * tok + lax.broadcasted_iota(jnp.int32, (1, tok), 1) - start
        row = jnp.floor((offset.astype(jnp.float32) + 0.5) / width.astype(jnp.float32))
        col = offset.astype(jnp.float32) - row * width.astype(jnp.float32)
        for half, place in enumerate((row, col)):
            angles = freq_ref[...] * place
            turns[2 * half] = jnp.cos(angles)
            turns[2 * half + 1] = jnp.sin(angles)
        for slot in range(3 * group):
            number = (seq - 1) * group + slot
            ids = ids_of(jnp.clip(number, 0, blocks - 1))
            outside = jnp.logical_or(number < 0, number >= blocks).astype(jnp.int32)
            key_seg[slot] = ids * (1 - outside) + count * outside

    def halo_start(j):
        @pl.when(has_right)
        def _():
            halo_copy(j, 0).start()

        @pl.when(has_left)
        def _():
            halo_copy(j, 1).start()

    def halo_arrive(j):
        @pl.when(has_left)
        def _():
            halo_copy(j, 0).wait_recv()

        @pl.when(has_right)
        def _():
            halo_copy(j, 1).wait_recv()

        @pl.when(jnp.logical_not(has_left))
        def _():
            for z in range(group):
                held[j, z] = jnp.zeros((3, HEAD, tok), jnp.bfloat16)

        @pl.when(jnp.logical_not(has_right))
        def _():
            for z in range(group):
                held[j, 2 * group + z] = jnp.zeros((3, HEAD, tok), jnp.bfloat16)

    def back_start(j, first=0, last=group):
        for d in partners:
            dest = partner(d)

            @pl.when(jnp.logical_and(dest >= first, dest < last))
            def _():
                back_copy(j, d).start()

        @pl.when(jnp.logical_and(me >= first, me < last))
        def _():
            back_own_copy(j).start()

    wide = 2 * tok
    lane = lax.broadcasted_iota(jnp.int32, (aug, tok), 0)

    def gather(j):
        for slot in range(3 * group):
            hot = jnp.where(key_seg[slot] == lane, 1.0, 0.0).astype(jnp.bfloat16)
            joined = jnp.concatenate([held[j, slot, 1], hot], axis=0)
            keys[pl.ds(slot * tok, tok)] = transposed(joined)
            values[:HEAD, pl.ds(slot * tok, tok)] = held[j, slot, 0]
        for z in range(group):
            queries[:HEAD, pl.ds(z * tok, tok)] = held[j, group + z, 2]

    def attend(j, first, last):
        def query_block(i, carry):
            base = i * wide
            q = queries[:, pl.ds(pl.multiple_of(base, 128), wide)]

            def key_block(step, state):
                top, acc = state
                start = pl.multiple_of(base + step * wide, 128)
                s = jnp.dot(keys[pl.ds(start, wide)], q, preferred_element_type=jnp.float32)
                new_top = jnp.maximum(top, jnp.max(s, axis=0, keepdims=True))
                weights = jnp.exp2((s - new_top) * scale).astype(jnp.bfloat16)
                acc = acc * jnp.exp2((top - new_top) * scale) + jnp.dot(
                    values[:, pl.ds(start, wide)], weights, preferred_element_type=jnp.float32
                )
                return new_top, acc

            top = jnp.full((1, wide), -1e30, jnp.float32)
            acc = jnp.zeros((HEAD + ONES, wide), jnp.float32)
            top, acc = lax.fori_loop(0, group + 1, key_block, (top, acc), unroll=True)
            mean = (acc[:HEAD] / acc[HEAD:HEAD + 1]).astype(jnp.bfloat16)
            blended[j, 2 * i] = mean[:, :tok]
            blended[j, 2 * i + 1] = mean[:, tok:]
            return carry

        lax.fori_loop(first, last, query_block, 0)

    prepare(0, 0)
    issue(0, 0)
    for j in range(1, chunks):
        for part in range(3):
            x_copy(j, part).start()
    lay_out()
    for part in (1, 2):
        prepare(0, part)
        issue(0, part)
    for part in range(3):
        prepare(1, part)
    values[HEAD:] = jnp.ones((ONES, values.shape[1]), jnp.bfloat16)
    for z in range(group):
        same = (key_seg[group + z] == lane) | (lane > count)
        queries[HEAD:, pl.ds(z * tok, tok)] = jnp.where(same, 0.0, APART).astype(jnp.bfloat16)

    pairs = group // 2

    def step(t, carry):
        @pl.when(t >= 1)
        def _():
            halo_arrive(t - 1)
            gather(t - 1)
            attend(t - 1, 0, pairs // 2)

        @pl.when(t == chunks)
        def _():
            back_start(t - 1, 0, pairs // 2 * 2)

        @pl.when(t < chunks)
        def _():
            arrive(t, 0)
            arrive(t, 1)
            halo_start(t)

        @pl.when(t + 1 < chunks)
        def _():
            for part in range(3):
                issue(t + 1, part)

        @pl.when(t == chunks - 1)
        def _():
            for j in range(chunks - 2):
                back_start(j)

        @pl.when(t >= 1)
        def _():
            attend(t - 1, pairs // 2, pairs)

        @pl.when(t < chunks)
        def _():
            arrive(t, 2)

        @pl.when(t == chunks - 1)
        def _():
            back_start(t - 1)

        @pl.when(t == chunks)
        def _():
            back_start(t - 1, pairs // 2 * 2, group)

        @pl.when(t + 2 < chunks)
        def _():
            for part in range(3):
                prepare(t + 2, part)

        return carry

    lax.fori_loop(0, chunks + 1, step, 0)

    def finish(j, carry):
        back_own_copy(j).wait()
        for d in partners:
            back_copy(j, d).wait_recv()
        cols = transposed(jnp.concatenate([back[j, z] for z in range(group)], axis=0))
        out_ref[:, pl.ds(pl.multiple_of(j * span, 128), span)] = cols
        for d in partners:
            for part in range(3):
                in_copy(j, d, part).wait_send()
            back_copy(j, d).wait_send()

        @pl.when(has_right)
        def _():
            halo_copy(j, 0).wait_send()

        @pl.when(has_left)
        def _():
            halo_copy(j, 1).wait_send()

        return carry

    lax.fori_loop(0, chunks, finish, 0)


def body(projected, segment_ids, widths):
    tok = projected.shape[0]
    group = lax.axis_size("head")
    seqs = lax.axis_size("seq")
    chunks = HEADS // group
    shard = tok * group
    count = widths.shape[0]
    aug = -(-(HEAD + count + 1) // 128) * 128 - HEAD
    frequency = 10000.0 ** (-np.arange(QUARTER, dtype=np.float64) / QUARTER)
    frequency = jnp.asarray(frequency.astype(np.float32))

    vmem = pl.BlockSpec(memory_space=pltpu.VMEM)
    dma = pltpu.SemaphoreType.DMA
    return pl.pallas_call(
        functools.partial(kernel, group, chunks, seqs, count),
        out_shape=jax.ShapeDtypeStruct((tok, D), jnp.bfloat16),
        in_specs=[
            pl.BlockSpec(memory_space=pl.ANY), vmem, pl.BlockSpec(memory_space=pltpu.SMEM), vmem
        ],
        out_specs=vmem,
        scratch_shapes=[
            pltpu.VMEM((chunks, 3, tok, group * HEAD), jnp.bfloat16),
            pltpu.VMEM((4, QUARTER, tok), jnp.float32),
            pltpu.VMEM((3 * group, 1, tok), jnp.int32),
            pltpu.VMEM((chunks, group, 3, HEAD, tok), jnp.bfloat16),
            pltpu.VMEM((chunks, 3 * group, 3, HEAD, tok), jnp.bfloat16),
            pltpu.VMEM((3 * shard, HEAD + aug), jnp.bfloat16),
            pltpu.VMEM((HEAD + ONES, 3 * shard), jnp.bfloat16),
            pltpu.VMEM((HEAD + aug, shard), jnp.bfloat16),
            pltpu.VMEM((chunks, group, HEAD, tok), jnp.bfloat16),
            pltpu.VMEM((chunks, group, HEAD, tok), jnp.bfloat16),
            dma((chunks, 3)),
            dma((chunks, group - 1, 3)),
            dma((chunks, group - 1, 3)),
            dma((chunks, 3)),
            dma((chunks, 2)),
            dma((chunks, 2)),
            dma((chunks, group - 1)),
            dma((chunks, group - 1)),
            dma((chunks,)),
        ],
        compiler_params=pltpu.CompilerParams(
            collective_id=0, has_side_effects=True, vmem_limit_bytes=56 * 2**20
        ),
        cost_estimate=pl.CostEstimate(
            flops=4 * shard * shard * 2 * D // group, bytes_accessed=tok * D * 8, transcendentals=0
        ),
    )(projected, frequency[:, None], widths, segment_ids.reshape(-1, 128 if tok % 128 == 0 else tok))


def solution(mesh):
    in_specs = (P(("seq", "head"), None), P(), P())
    out_specs = P(("seq", "head"), None)
    return jax.shard_map(body, mesh=mesh, in_specs=in_specs, out_specs=out_specs, check_vma=False)
```
